32 devices in a mesh: grp: 2 (over x), lon: 16 (over z, y, core).
Axes of the slice: x: 2, y: 2, z: 4, core: 2. Of those that a mesh axis runs over, the one named last changes fastest.
Arguments:
- adjoint_final: float32 [80, 16, 32, 128], P('grp', None, 'lon'), parts along dimension 0, may hold values from -6 to 6
- winds: float32 [4, 2, 16, 128, 32], P(None, None, None, 'lon'), may hold values from -0.4 to 0.4
- diffusivity: float32 [15, 32, 128], P(None, 'lon'), may hold values from 0.02 to 0.24
- observed_values: float32 [8192, 640], P(('grp', 'lon')), parts along dimension 0, may hold values from -6 to 6
- observed_band: int32 [8192, 1], P(('grp', 'lon')), parts along dimension 0, may hold values from 0 to 15; in each aligned block of 256 rows (0 to 255, 256 to 511, ...) at most 32 rows name the same one
- observed_cell: int32 [8192], P(('grp', 'lon')), parts along dimension 0, may hold values from 0 to 255
- observed_step: int32 [8192], P(('grp', 'lon')), parts along dimension 0, may hold values from 0 to 3
Outputs:
- adjoint_start: float32 [80, 16, 32, 128], P('grp', None, 'lon'), parts along dimension 0
- flux_sensitivity: float32 [80, 32, 128], P('grp', 'lon'), parts along dimension 0
The draws below stay inside these ranges and needn't reach their ends.
There are 2 independent parts, one for each index of `grp`. The reference program is written for one: setup_inputs(seed, part) draws one part's arguments, and reference() takes and returns one part's arrays. A program takes and returns all parts, laid end to end along the dimension named above; an argument that names none is the same for every part. Nothing has to cross between parts.
Inputs may be any that keep to these rules, and one draw needn't show every extreme that they name: `observed_band`: among the observation rows of one device no band is named more than 32 times, a bound that some block reaches.
All inputs are finite; a program needn't handle non-finite values.
Results may differ from the reference program's by a relative error of at most 0.0003.
Values sent between devices are 32-bit elements; how exact they have to be, the bound alone decides.
A program may use at most 64 MiB of HBM per device.

```python
import math
import jax
import jax.numpy as jnp
import numpy as np
from jax import lax

TR = 40
LEV = 16
LAT = 128
LON_DEV = 2
STEPS = 4
SUB = 4
OBS_DEV = 256
NLON = 32
LEVM = 15
OBS = 4096
CAP = 32
N_LON = 16


def with_ends(values, key, low, top_value):
    dims = values.shape
    index_at = [jax.random.randint(jax.random.fold_in(key, axis), (), 0, dims[axis]) for axis in range(len(dims))]
    values = values.at[tuple(index_at)].set(low)
    longest = dims.index(max(dims))
    index_at[longest] = (index_at[longest] + 1) % dims[longest]
    return values.at[tuple(index_at)].set(top_value)


def block_levels(own_key, dims, shards, low, top_value):
    loudness = 1.0
    for position, blocks in shards:
        steps = jax.random.uniform(jax.random.fold_in(jax.random.fold_in(own_key, 6), position), (blocks,), jnp.float32, low / len(shards), top_value / len(shards))
        loudness = loudness * jnp.repeat(jnp.exp(steps), dims[position] // blocks).reshape((-1,) + (1,) * (len(dims) - 1 - position))
    return loudness


def routed_block(key, own, number, rows, amount, top, most, lean):
    ranking = jax.random.permutation(key, amount)
    heavy_load, common = shares(amount, rows * top, most, lean, True), shares(amount, rows * top, most, lean, False)
    places = jnp.arange(amount)

    def named(sizes, offset_by):
        used = int((sizes > 0).sum())
        fixed = max(1, used // 4)
        passed = fixed + (places - fixed + offset_by * (used - fixed)) % max(1, amount - fixed)
        return jnp.zeros((amount,), jnp.int32).at[ranking[jnp.where(places < fixed, places, passed)]].set(jnp.asarray(sizes, jnp.int32))

    sizes = jnp.where(number % 4 == 0, named(heavy_load, number // 4), named(common, number - number // 4 - 1))
    mixed = jax.random.permutation(jax.random.fold_in(own, 3), amount)
    donor, sink = mixed[0:amount // 2 * 2:2], mixed[1:amount // 2 * 2:2]
    room = jnp.minimum(sizes[donor] - 1, most - sizes[sink]) // 2
    room = jnp.where((donor == ranking[0]) | (sink == ranking[0]) | (sizes[sink] == 0), 0, jnp.maximum(room, 0))
    passed = jax.random.randint(jax.random.fold_in(own, 4), (amount // 2,), 0, 1 << 20) % (room + 1)
    sizes = sizes.at[donor].add(-passed).at[sink].add(passed)
    members = jnp.searchsorted(jnp.cumsum(sizes), jnp.arange(rows * top), side="right").astype(jnp.int32)
    grid = members.reshape(top, rows).T
    grid = grid[jax.random.permutation(jax.random.fold_in(own, 1), rows)]
    offset_by = jax.random.randint(jax.random.fold_in(own, 2), (rows, 1), 0, top)
    return jnp.take_along_axis(grid, (jnp.arange(top)[None, :] + offset_by) % top, axis=1)


def shares(number_of, total, reach, skew, full):
    portions = [(1 << 20) // math.isqrt(rank ** skew) + 1 for rank in range(1, number_of + 1)]
    largest = reach if full else min(reach, max(-(-total // number_of), total * portions[0] // sum(portions)))
    least = 1 if total - largest >= number_of - 1 else 0
    holding, surplus = [largest] + [least] * (number_of - 1), total - largest - least * (number_of - 1)
    while surplus > 0:
        candidates = [i for i in range(1, number_of) if holding[i] < largest] or [i for i in range(1, number_of) if holding[i] < reach]
        mass, left = sum([portions[i] for i in candidates]), surplus
        for i in candidates:
            addition = min(reach - holding[i], max(1, left * portions[i] // mass), surplus)
            holding[i] = holding[i] + addition
            surplus = surplus - addition
    return np.array(holding)


def centred(own_key, dims, deviation, reach, shards=(), kind=jnp.bfloat16):
    entries = jax.random.normal(own_key, dims, jnp.float32) * deviation
    if len(shards) > 0:
        entries = block_levels(own_key, dims, shards, -0.22, 0.18) * entries
    return jnp.clip(entries, min=-reach, max=reach).astype(kind)


def setup_inputs(seed: int = 0, part: int = 0) -> dict:
    streams_of = jax.random.split(jax.random.key(seed), 8)
    part_keys = jax.random.split(jax.random.fold_in(streams_of[7], part), 8)
    adjoint_final = centred(part_keys[0], (TR, LEV, NLON, LAT), 1.0, 6.0, ((2, 16),), jnp.float32)
    winds = jnp.clip(jax.random.uniform(streams_of[1], (STEPS, 2, LEV, LAT, NLON), jnp.float32, -0.4, 0.4) * block_levels(streams_of[1], (STEPS, 2, LEV, LAT, NLON), ((3, 16),), -0.4, 0.0), -0.4, 0.4)
    diffusivity = jnp.clip(jnp.exp(math.log(0.24) - 2.4849066 * jax.random.uniform(streams_of[2], (LEVM, NLON, LAT), jnp.float32) ** block_levels(streams_of[2], (LEVM, NLON, LAT), ((1, 16),), -0.2, 0.2)), 0.02, 0.24)
    observed_values = centred(part_keys[3], (OBS, TR * LEV), 1.0, 6.0, ((0, 16),), jnp.float32)
    observed_band_keys = jax.random.split(jax.random.fold_in(part_keys[4], 1), OBS // OBS_DEV)
    observed_band_turns = jax.random.permutation(jax.random.fold_in(part_keys[4], 3), OBS // OBS_DEV)
    observed_band = jax.vmap(lambda own, number: routed_block(jax.random.fold_in(part_keys[4], 2), own, number, OBS_DEV, N_LON, 1, CAP, 2))(observed_band_keys, observed_band_turns).reshape((OBS, 1))
    observed_cell = with_ends(jax.random.randint(part_keys[5], (OBS,), 0, LON_DEV * LAT), jax.random.fold_in(part_keys[5], 1), 0, (LON_DEV * LAT) - 1).astype(jnp.int32)
    observed_step = with_ends(jax.random.randint(part_keys[6], (OBS,), 0, STEPS), jax.random.fold_in(part_keys[6], 1), 0, STEPS - 1).astype(jnp.int32)
    return dict(adjoint_final=adjoint_final, winds=winds, diffusivity=diffusivity, observed_values=observed_values, observed_band=observed_band, observed_cell=observed_cell, observed_step=observed_step)


def shift_zero(values_in, offset, along_axis):
    length = values_in.shape[along_axis]
    pad_shape = list(values_in.shape)
    pad_shape[along_axis] = abs(offset)
    zero_rim = jnp.zeros(pad_shape, values_in.dtype)
    if offset > 0:
        kept_part = lax.slice_in_dim(values_in, offset, length, axis=along_axis)
        return jnp.concatenate([kept_part, zero_rim], axis=along_axis)
    kept_part = lax.slice_in_dim(values_in, 0, length + offset, axis=along_axis)
    return jnp.concatenate([zero_rim, kept_part], axis=along_axis)

def upwind_weights(courant):
    magnitude = jnp.abs(courant)
    return ((-2, -(courant + magnitude) / 12.0), (-1, (8.0 * courant + 4.0 * magnitude) / 12.0), (1, (4.0 * magnitude - 8.0 * courant) / 12.0), (2, (courant - magnitude) / 12.0))

def diffuse(tracer_field, rate_field, level_axis):
    count = tracer_field.shape[level_axis]
    for substep in range(SUB):
        upper_levels = lax.slice_in_dim(tracer_field, 1, count, axis=level_axis)
        lower_levels = lax.slice_in_dim(tracer_field, 0, count - 1, axis=level_axis)
        flux_term = rate_field * (upper_levels - lower_levels)
        pad_shape = list(tracer_field.shape)
        pad_shape[level_axis] = 1
        zero_rim = jnp.zeros(pad_shape, tracer_field.dtype)
        tracer_field = tracer_field + jnp.concatenate([flux_term, zero_rim], axis=level_axis) - jnp.concatenate([zero_rim, flux_term], axis=level_axis)
    return tracer_field

def forward_step(tracer_field, wind_x, wind_y, rate_field):
    result = (1.0 - 0.5 * jnp.abs(wind_x) - 0.5 * jnp.abs(wind_y)) * tracer_field
    for offset, weight in upwind_weights(wind_x):
        result = result + weight * jnp.roll(tracer_field, -offset, axis=1)
    for offset, weight in upwind_weights(wind_y):
        result = result + weight * shift_zero(tracer_field, offset, 2)
    return diffuse(result, rate_field, 0)

def reference(adjoint_final, winds, diffusivity, observed_values, observed_band, observed_cell, observed_step):
    wind_all = jnp.swapaxes(winds, 3, 4)
    global_lon = (observed_band[:, 0] * LON_DEV + observed_cell // LAT).astype(jnp.int32)
    global_lat = (observed_cell % LAT).astype(jnp.int32)

    def per_tracer(tracer):
        start = (tracer * LEV).astype(jnp.int32)
        values = lax.dynamic_slice_in_dim(observed_values, start, LEV, 1)
        adjoint = lax.dynamic_index_in_dim(adjoint_final, tracer, 0, keepdims=False)
        flux_sum = jnp.zeros((NLON, LAT), jnp.float32)
        for step_index in reversed(range(STEPS)):
            selected = jnp.where((observed_step == step_index)[:, None], values, jnp.zeros_like(values))
            forcing = jnp.zeros((LEV, NLON, LAT), jnp.float32).at[:, global_lon, global_lat].add(selected.T)
            adjoint = adjoint + forcing
            wind_x = wind_all[step_index, 0]
            wind_y = wind_all[step_index, 1]

            def step_map(tracer_field):
                return forward_step(tracer_field, wind_x, wind_y, diffusivity)
            result, pullback = jax.vjp(step_map, adjoint)
            adjoint = pullback(adjoint)[0]
            flux_sum = flux_sum + adjoint[0]
        return (adjoint, flux_sum)
    fields, fluxes = lax.map(per_tracer, jnp.arange(TR, dtype=jnp.int32))
    return (fields, fluxes)
```

```python
import functools

import jax
import jax.numpy as jnp
from jax import lax
from jax.experimental import pallas as pl
from jax.experimental.pallas import tpu as pltpu
from jax.sharding import PartitionSpec as P

SUB = 4
ROWS = 8


def chunk_sizes(tracers):
    units = tracers // ROWS
    first = (units + 1) // 2
    return [n * ROWS for n in (first, units - first) if n]


def shifted(block, axis, distance):
    devices = range(lax.axis_size(axis))
    route = [((i - distance) % len(devices), i) for i in devices]
    return lax.ppermute(block, axis, route)


def step_weights(winds):
    u, v = winds[:, 0], winds[:, 1]

    def upwind(c):
        m = jnp.abs(c)
        return [
            -(c + m) / 12.0,
            (8.0 * c + 4.0 * m) / 12.0,
            (4.0 * m - 8.0 * c) / 12.0,
            (c - m) / 12.0,
        ]

    lat = winds.shape[-1]
    place = jnp.arange(lat)
    inside = [
        jnp.where((place + k >= 0) & (place + k < lat), w, 0.0)
        for k, w in zip((-2, -1, 1, 2), upwind(v))
    ]
    centre = 1.0 - 0.5 * jnp.abs(u) - 0.5 * jnp.abs(v)
    return jnp.stack([centre] + inside + upwind(u), axis=1)


def step_kernel(halo, *refs):
    if halo:
        q_ref, west_ref, east_ref, flux_ref, f_ref, w_ref, r_ref = refs[:7]
        out_ref, oeast_ref, owest_ref, oflux_ref = refs[7:]
    else:
        q_ref, f_ref, w_ref, r_ref = refs[:4]
        out_ref, oeast_ref, owest_ref = refs[4:]
    levels, columns, tracers, lat = q_ref.shape

    @pl.loop(0, tracers // ROWS)
    def _(i):
        at = pl.ds(pl.multiple_of(i * ROWS, ROWS), ROWS)
        field = []
        for x in range(columns):
            q = [q_ref[l, x, at, :] for l in range(levels)]
            if halo:
                q = [q[l] + (west_ref[l, x, at, :] + east_ref[l, x, at, :]) for l in range(levels)]
                oflux_ref[x, at, :] = flux_ref[x, at, :] + q[0]
            q = [q[l] + f_ref[l, x, at, :] for l in range(levels)]
            for _ in range(SUB):
                flow = [r_ref[l, x : x + 1, :] * (q[l + 1] - q[l]) for l in range(levels - 1)]
                q = (
                    [q[0] + flow[0]]
                    + [q[l] + flow[l] - flow[l - 1] for l in range(1, levels - 1)]
                    + [q[levels - 1] - flow[levels - 2]]
                )
            for l in range(levels):
                out_ref[l, x, at, :] = q[l]
        for l in range(levels):
            q = [out_ref[l, x, at, :] for x in range(columns)]

            def w(k, x):
                return w_ref[k, l, x : x + 1, :]

            total = []
            for x in range(columns):
                t = w(0, x) * q[x]
                for k, offset in ((1, -2), (2, -1), (3, 1), (4, 2)):
                    t = t + pltpu.roll(w(k, x) * q[x], offset % lat, 1)
                total.append(t)
            last = columns - 1
            for k, offset in ((5, -2), (6, -1), (7, 1), (8, 2)):
                for x in range(columns):
                    if 0 <= x + offset < columns:
                        total[x + offset] = total[x + offset] + w(k, x) * q[x]
            for x in range(columns):
                out_ref[l, x, at, :] = total[x]
            oeast_ref[l, 0, at, :] = w(7, last) * q[last] + w(8, last - 1) * q[last - 1]
            oeast_ref[l, 1, at, :] = w(8, last) * q[last]
            owest_ref[l, 0, at, :] = w(5, 0) * q[0]
            owest_ref[l, 1, at, :] = w(6, 0) * q[0] + w(5, 1) * q[1]


def step(q, halos, flux, forcing, weights, rate):
    levels, columns, tracers, lat = q.shape
    whole = jax.ShapeDtypeStruct(q.shape, jnp.float32)
    edge = jax.ShapeDtypeStruct((levels, 2, tracers, lat), jnp.float32)
    outs = [whole, edge, edge]
    operands = [q]
    if halos:
        operands += [halos[0], halos[1], flux]
        outs.append(jax.ShapeDtypeStruct(flux.shape, jnp.float32))
    operands += [forcing, weights, rate]
    vmem = pl.BlockSpec(memory_space=pltpu.VMEM)
    size = q.size
    return pl.pallas_call(
        functools.partial(step_kernel, bool(halos)),
        out_shape=outs,
        in_specs=[vmem] * len(operands),
        out_specs=[vmem] * len(outs),
        compiler_params=pltpu.CompilerParams(vmem_limit_bytes=24 << 20),
        cost_estimate=pl.CostEstimate(flops=60 * size, bytes_accessed=32 * size, transcendentals=0),
    )(*operands)


def split(values):
    high = lax.reduce_precision(values, 8, 7)
    return high.astype(jnp.bfloat16), (values - high).astype(jnp.bfloat16)


def select(hot, values):
    high, low = split(values)
    dims = (((0,), (0,)), ((), ()))
    dot = functools.partial(
        lax.dot_general, dimension_numbers=dims, preferred_element_type=jnp.float32
    )
    return dot(hot, high) + dot(hot, low)


def body(
    adjoint_final, winds, diffusivity, observed_values, observed_band, observed_cell, observed_step
):
    tracers, levels, columns, lat = adjoint_final.shape
    steps = winds.shape[0]
    rows, payload = observed_values.shape
    bands = lax.axis_size("lon")
    capacity = max(2, (2 * rows + bands - 1) // bands)
    cells = columns * lat

    target = observed_band[:, 0]
    named = target[:, None] == jnp.arange(bands, dtype=jnp.int32)[None, :]
    counted = named.astype(jnp.float32)
    earlier = (jnp.arange(rows)[:, None] > jnp.arange(rows)[None, :]).astype(jnp.float32)
    before = jnp.dot(earlier, counted, preferred_element_type=jnp.float32)
    slot = jnp.sum(before * counted, axis=1).astype(jnp.int32)
    place = target * capacity + slot
    hot = place[:, None] == jnp.arange(bands * capacity, dtype=jnp.int32)[None, :]
    code = (observed_step * cells + observed_cell).astype(jnp.float32)
    send_code = jnp.sum(jnp.where(hot, code[:, None] + 1.0, 0.0), axis=0) - 1.0
    send_values = select(hot.astype(jnp.bfloat16), observed_values)

    lat_rows = winds.shape[3]
    parts = winds.reshape(steps * 2 * levels * lat_rows, bands, columns).transpose(1, 0, 2)
    small = jnp.concatenate(
        [parts.reshape(bands, -1), send_code.reshape(bands, capacity)], axis=1
    )
    small = lax.all_to_all(small, "lon", split_axis=0, concat_axis=0, tiled=True)
    recv_values = lax.all_to_all(send_values, "lon", split_axis=0, concat_axis=0, tiled=True)
    recv_code = small[:, -capacity:].reshape(-1).astype(jnp.int32)
    own = small[:, :-capacity].reshape(bands, steps, 2, levels, lat_rows, columns)
    own = own.transpose(1, 2, 3, 5, 0, 4).reshape(steps, 2, levels, columns, lat)
    weights = step_weights(own)

    by_level = recv_values.reshape(-1, tracers, levels).transpose(0, 2, 1).reshape(-1, payload)
    high, low = split(by_level)
    cell_hot = (
        recv_code[:, None] == jnp.arange(steps * cells, dtype=jnp.int32)[None, :]
    ).astype(jnp.bfloat16)
    cell_hot = cell_hot.reshape(-1, steps * columns, lat)

    def dot(part):
        return jnp.einsum("kp,ksy->spy", part, cell_hot, preferred_element_type=jnp.float32)

    forcing = (dot(high) + dot(low)).reshape(steps, columns, levels, tracers, lat)
    forcing = forcing.transpose(0, 2, 1, 3, 4)

    field = adjoint_final.transpose(1, 2, 0, 3)
    ends = []
    start = 0
    for size in chunk_sizes(tracers):
        ends.append((start, start + size))
        start += size
    states = [(field[:, :, a:b], None, None) for a, b in ends]
    for number, s in enumerate(reversed(range(steps))):
        moved = []
        for (a, b), (q, halos, flux) in zip(ends, states):
            if number == 1:
                flux = jnp.zeros((columns, b - a, lat), jnp.float32)
            out = step(q, halos, flux, forcing[s, :, :, a:b], weights[s], diffusivity)
            halos = (shifted(out[1], "lon", 1), shifted(out[2], "lon", -1))
            moved.append((out[0], halos, out[3] if number else None))
        states = moved
    fields, fluxes = [], []
    for q, halos, flux in states:
        q = q.at[:, 0:2].add(halos[0])
        q = q.at[:, columns - 2 : columns].add(halos[1])
        fields.append(q)
        fluxes.append(flux + q[0])
    field = jnp.concatenate(fields, axis=2).transpose(2, 0, 1, 3)
    return field, jnp.concatenate(fluxes, axis=1).transpose(1, 0, 2)


def solution(mesh):
    return jax.shard_map(
        body,
        mesh=mesh,
        in_specs=(
            P("grp", None, "lon", None),
            P(None, None, None, "lon", None),
            P(None, "lon", None),
            P(("grp", "lon"), None),
            P(("grp", "lon"), None),
            P(("grp", "lon")),
            P(("grp", "lon")),
        ),
        out_specs=(P("grp", None, "lon", None), P("grp", "lon", None)),
        check_vma=False,
    )
```

```python
import functools

import jax
import jax.numpy as jnp
from jax import lax
from jax.experimental import pallas as pl
from jax.experimental.pallas import tpu as pltpu
from jax.sharding import PartitionSpec as P

SUB = 4
ROWS = 8


def chunk_sizes(tracers):
    units = tracers // ROWS
    first = (units + 1) // 2
    return [n * ROWS for n in (first, units - first) if n]


def shifted(block, axis, distance):
    devices = range(lax.axis_size(axis))
    route = [((i - distance) % len(devices), i) for i in devices]
    return lax.ppermute(block, axis, route)


def step_weights(winds):
    u, v = winds[:, 0], winds[:, 1]

    def upwind(c):
        m = jnp.abs(c)
        return [
            -(c + m) / 12.0,
            (8.0 * c + 4.0 * m) / 12.0,
            (4.0 * m - 8.0 * c) / 12.0,
            (c - m) / 12.0,
        ]

    lat = winds.shape[-1]
    place = jnp.arange(lat)
    inside = [
        jnp.where((place + k >= 0) & (place + k < lat), w, 0.0)
        for k, w in zip((-2, -1, 1, 2), upwind(v))
    ]
    centre = 1.0 - 0.5 * jnp.abs(u) - 0.5 * jnp.abs(v)
    return jnp.stack([centre] + inside + upwind(u), axis=1)


def step_kernel(halo, start, *refs):
    if halo:
        q_ref, west_ref, east_ref, flux_ref, f_ref, w_ref, r_ref = refs[:7]
        out_ref, oeast_ref, owest_ref, oflux_ref = refs[7:]
    else:
        q_ref, f_ref, w_ref, r_ref = refs[:4]
        out_ref, oeast_ref, owest_ref = refs[4:]
    levels, columns, tracers, lat = q_ref.shape

    @pl.loop(0, tracers // ROWS)
    def _(i):
        at = pl.ds(pl.multiple_of(i * ROWS, ROWS), ROWS)
        own = pl.ds(pl.multiple_of(start + i * ROWS, ROWS), ROWS)
        for x in range(columns):
            q = [q_ref[l, x, at, :] for l in range(levels)]
            if halo:
                q = [q[l] + (west_ref[l, x, at, :] + east_ref[l, x, at, :]) for l in range(levels)]
                oflux_ref[x, at, :] = flux_ref[x, at, :] + q[0]
            q = [q[l] + f_ref[x, l, own, :] for l in range(levels)]
            for _ in range(SUB):
                flow = [r_ref[l, x : x + 1, :] * (q[l + 1] - q[l]) for l in range(levels - 1)]
                q = (
                    [q[0] + flow[0]]
                    + [q[l] + flow[l] - flow[l - 1] for l in range(1, levels - 1)]
                    + [q[levels - 1] - flow[levels - 2]]
                )
            for l in range(levels):
                out_ref[l, x, at, :] = q[l]
        for l in range(levels):
            q = [out_ref[l, x, at, :] for x in range(columns)]

            def w(k, x):
                return w_ref[k, l, x : x + 1, :]

            total = []
            for x in range(columns):
                t = w(0, x) * q[x]
                for k, offset in ((1, -2), (2, -1), (3, 1), (4, 2)):
                    t = t + pltpu.roll(w(k, x) * q[x], offset % lat, 1)
                total.append(t)
            last = columns - 1
            for k, offset in ((5, -2), (6, -1), (7, 1), (8, 2)):
                for x in range(columns):
                    if 0 <= x + offset < columns:
                        total[x + offset] = total[x + offset] + w(k, x) * q[x]
            for x in range(columns):
                out_ref[l, x, at, :] = total[x]
            oeast_ref[l, 0, at, :] = w(7, last) * q[last] + w(8, last - 1) * q[last - 1]
            oeast_ref[l, 1, at, :] = w(8, last) * q[last]
            owest_ref[l, 0, at, :] = w(5, 0) * q[0]
            owest_ref[l, 1, at, :] = w(6, 0) * q[0] + w(5, 1) * q[1]


def step(q, halos, flux, forcing, weights, rate, start):
    levels, columns, tracers, lat = q.shape
    whole = jax.ShapeDtypeStruct(q.shape, jnp.float32)
    edge = jax.ShapeDtypeStruct((levels, 2, tracers, lat), jnp.float32)
    outs = [whole, edge, edge]
    operands = [q]
    if halos:
        operands += [halos[0], halos[1], flux]
        outs.append(jax.ShapeDtypeStruct(flux.shape, jnp.float32))
    operands += [forcing, weights, rate]
    vmem = pl.BlockSpec(memory_space=pltpu.VMEM)
    size = q.size
    return pl.pallas_call(
        functools.partial(step_kernel, bool(halos), start),
        out_shape=outs,
        in_specs=[vmem] * len(operands),
        out_specs=[vmem] * len(outs),
        compiler_params=pltpu.CompilerParams(vmem_limit_bytes=24 << 20),
        cost_estimate=pl.CostEstimate(flops=60 * size, bytes_accessed=32 * size, transcendentals=0),
    )(*operands)


def forcing_kernel(first, code_ref, high_ref, low_ref, out_ref):
    columns, _, lat = out_ref.shape
    for x in range(columns):
        cell = first + x * lat + lax.broadcasted_iota(jnp.int32, (code_ref.shape[0], lat), 1)
        hot = jnp.where(code_ref[...] == cell, 1.0, 0.0).astype(jnp.bfloat16)
        total = jnp.dot(high_ref[...], hot, preferred_element_type=jnp.float32)
        out_ref[x] = total + jnp.dot(low_ref[...], hot, preferred_element_type=jnp.float32)


def step_forcing(code, high, low, first, columns, lat):
    payload, slots = high.shape
    vmem = pl.BlockSpec(memory_space=pltpu.VMEM)
    return pl.pallas_call(
        functools.partial(forcing_kernel, first),
        out_shape=jax.ShapeDtypeStruct((columns, payload, lat), jnp.float32),
        in_specs=[vmem] * 3,
        out_specs=vmem,
        compiler_params=pltpu.CompilerParams(vmem_limit_bytes=24 << 20),
        cost_estimate=pl.CostEstimate(
            flops=4 * payload * slots * columns * lat,
            bytes_accessed=4 * payload * (slots + columns * lat),
            transcendentals=0,
        ),
    )(code, high, low)


def split(values):
    high = lax.reduce_precision(values, 8, 7)
    return high.astype(jnp.bfloat16), (values - high).astype(jnp.bfloat16)


def body(
    adjoint_final, winds, diffusivity, observed_values, observed_band, observed_cell, observed_step
):
    tracers, levels, columns, lat = adjoint_final.shape
    steps = winds.shape[0]
    rows, payload = observed_values.shape
    bands = lax.axis_size("lon")
    capacity = max(2, (2 * rows + bands - 1) // bands)
    cells = columns * lat

    target = observed_band[:, 0]
    named = target[:, None] == jnp.arange(bands, dtype=jnp.int32)[None, :]
    counted = named.astype(jnp.float32)
    earlier = (jnp.arange(rows)[:, None] > jnp.arange(rows)[None, :]).astype(jnp.float32)
    before = jnp.dot(earlier, counted, preferred_element_type=jnp.float32)
    slot = jnp.sum(before * counted, axis=1).astype(jnp.int32)
    place = target * capacity + slot
    hot = place[:, None] == jnp.arange(bands * capacity, dtype=jnp.int32)[None, :]
    code = (observed_step * cells + observed_cell).astype(jnp.float32)
    send_code = jnp.sum(jnp.where(hot, code[:, None] + 1.0, 0.0), axis=0) - 1.0
    column = jnp.arange(payload, dtype=jnp.int32)
    source = (column % tracers) * levels + column // tracers
    swap = (column[:, None] == source[None, :]).astype(jnp.bfloat16)
    high, low = split(observed_values)
    dims = (((0,), (0,)), ((), ()))
    send_values = 0.0
    for part in (high, low):
        part = jnp.dot(part, swap, preferred_element_type=jnp.float32).astype(jnp.bfloat16)
        send_values = send_values + lax.dot_general(
            hot.astype(jnp.bfloat16), part, dims, preferred_element_type=jnp.float32
        )

    lat_rows = winds.shape[3]
    parts = winds.reshape(steps * 2 * levels * lat_rows, bands, columns).transpose(1, 0, 2)
    small = jnp.concatenate(
        [parts.reshape(bands, -1), send_code.reshape(bands, capacity)], axis=1
    )
    small = lax.all_to_all(small, "lon", split_axis=0, concat_axis=0, tiled=True)
    recv_values = lax.all_to_all(send_values, "lon", split_axis=0, concat_axis=0, tiled=True)
    recv_code = small[:, -capacity:].reshape(-1).astype(jnp.int32)
    own = small[:, :-capacity].reshape(bands, steps, 2, levels, lat_rows, columns)
    own = own.transpose(1, 2, 3, 5, 0, 4).reshape(steps, 2, levels, columns, lat)
    weights = step_weights(own)

    high, low = split(recv_values.T)
    code = recv_code[:, None]

    field = adjoint_final.transpose(1, 2, 0, 3)
    ends = []
    start = 0
    for size in chunk_sizes(tracers):
        ends.append((start, start + size))
        start += size
    states = [(field[:, :, a:b], None, None) for a, b in ends]
    for number, s in enumerate(reversed(range(steps))):
        moved = []
        forcing = step_forcing(code, high, low, s * cells, columns, lat)
        forcing = forcing.reshape(columns, levels, tracers, lat)
        for (a, b), (q, halos, flux) in zip(ends, states):
            if number == 1:
                flux = jnp.zeros((columns, b - a, lat), jnp.float32)
            out = step(q, halos, flux, forcing, weights[s], diffusivity, a)
            halos = (shifted(out[1], "lon", 1), shifted(out[2], "lon", -1))
            moved.append((out[0], halos, out[3] if number else None))
        states = moved
    fields, fluxes = [], []
    for q, halos, flux in states:
        q = q.at[:, 0:2].add(halos[0])
        q = q.at[:, columns - 2 : columns].add(halos[1])
        fields.append(q)
        fluxes.append(flux + q[0])
    field = jnp.concatenate(fields, axis=2).transpose(2, 0, 1, 3)
    return field, jnp.concatenate(fluxes, axis=1).transpose(1, 0, 2)


def solution(mesh):
    return jax.shard_map(
        body,
        mesh=mesh,
        in_specs=(
            P("grp", None, "lon", None),
            P(None, None, None, "lon", None),
            P(None, "lon", None),
            P(("grp", "lon"), None),
            P(("grp", "lon"), None),
            P(("grp", "lon")),
            P(("grp", "lon")),
        ),
        out_specs=(P("grp", None, "lon", None), P("grp", "lon", None)),
        check_vma=False,
    )
```

```python
import functools

import jax
import jax.numpy as jnp
from jax import lax
from jax.experimental import pallas as pl
from jax.experimental.pallas import tpu as pltpu
from jax.sharding import PartitionSpec as P

SUB = 4
ROWS = 8


def chunk_sizes(tracers):
    units = tracers // ROWS
    first = (units + 1) // 2
    return [n * ROWS for n in (first, units - first) if n]


def shifted(block, axis, distance):
    devices = range(lax.axis_size(axis))
    route = [((i - distance) % len(devices), i) for i in devices]
    return lax.ppermute(block, axis, route)


def step_weights(winds):
    u, v = winds[:, 0], winds[:, 1]

    def upwind(c):
        m = jnp.abs(c)
        return [
            -(c + m) / 12.0,
            (8.0 * c + 4.0 * m) / 12.0,
            (4.0 * m - 8.0 * c) / 12.0,
            (c - m) / 12.0,
        ]

    lat = winds.shape[-1]
    place = jnp.arange(lat)
    inside = [
        jnp.where((place + k >= 0) & (place + k < lat), w, 0.0)
        for k, w in zip((-2, -1, 1, 2), upwind(v))
    ]
    centre = 1.0 - 0.5 * jnp.abs(u) - 0.5 * jnp.abs(v)
    return jnp.stack([centre] + inside + upwind(u), axis=1)


def step_kernel(halo, start, *refs):
    if halo:
        q_ref, west_ref, east_ref, flux_ref, f_ref, w_ref, r_ref = refs[:7]
        out_ref, oeast_ref, owest_ref, oflux_ref = refs[7:]
    else:
        q_ref, f_ref, w_ref, r_ref = refs[:4]
        out_ref, oeast_ref, owest_ref = refs[4:]
    levels, columns, tracers, lat = q_ref.shape

    @pl.loop(0, tracers // ROWS)
    def _(i):
        at = pl.ds(pl.multiple_of(i * ROWS, ROWS), ROWS)
        own = pl.ds(pl.multiple_of(start + i * ROWS, ROWS), ROWS)
        for x in range(columns):
            q = [q_ref[l, x, at, :] for l in range(levels)]
            if halo:
                q = [q[l] + (west_ref[l, x, at, :] + east_ref[l, x, at, :]) for l in range(levels)]
                oflux_ref[x, at, :] = flux_ref[x, at, :] + q[0]
            q = [q[l] + f_ref[x, l, own, :] for l in range(levels)]
            for _ in range(SUB):
                flow = [r_ref[l, x : x + 1, :] * (q[l + 1] - q[l]) for l in range(levels - 1)]
                q = (
                    [q[0] + flow[0]]
                    + [q[l] + flow[l] - flow[l - 1] for l in range(1, levels - 1)]
                    + [q[levels - 1] - flow[levels - 2]]
                )
            for l in range(levels):
                out_ref[l, x, at, :] = q[l]
        for l in range(levels):
            q = [out_ref[l, x, at, :] for x in range(columns)]

            def w(k, x):
                return w_ref[k, l, x : x + 1, :]

            total = []
            for x in range(columns):
                t = w(0, x) * q[x]
                for k, offset in ((1, -2), (2, -1), (3, 1), (4, 2)):
                    t = t + pltpu.roll(w(k, x) * q[x], offset % lat, 1)
                total.append(t)
            last = columns - 1
            for k, offset in ((5, -2), (6, -1), (7, 1), (8, 2)):
                for x in range(columns):
                    if 0 <= x + offset < columns:
                        total[x + offset] = total[x + offset] + w(k, x) * q[x]
            for x in range(columns):
                out_ref[l, x, at, :] = total[x]
            oeast_ref[l, 0, at, :] = w(7, last) * q[last] + w(8, last - 1) * q[last - 1]
            oeast_ref[l, 1, at, :] = w(8, last) * q[last]
            owest_ref[l, 0, at, :] = w(5, 0) * q[0]
            owest_ref[l, 1, at, :] = w(6, 0) * q[0] + w(5, 1) * q[1]


def step(q, halos, flux, forcing, weights, rate, start):
    levels, columns, tracers, lat = q.shape
    whole = jax.ShapeDtypeStruct(q.shape, jnp.float32)
    edge = jax.ShapeDtypeStruct((levels, 2, tracers, lat), jnp.float32)
    outs = [whole, edge, edge]
    operands = [q]
    if halos:
        operands += [halos[0], halos[1], flux]
        outs.append(jax.ShapeDtypeStruct(flux.shape, jnp.float32))
    operands += [forcing, weights, rate]
    vmem = pl.BlockSpec(memory_space=pltpu.VMEM)
    size = q.size
    return pl.pallas_call(
        functools.partial(step_kernel, bool(halos), start),
        out_shape=outs,
        in_specs=[vmem] * len(operands),
        out_specs=[vmem] * len(outs),
        compiler_params=pltpu.CompilerParams(vmem_limit_bytes=24 << 20),
        cost_estimate=pl.CostEstimate(flops=60 * size, bytes_accessed=32 * size, transcendentals=0),
    )(*operands)


def forcing_kernel(first, code_ref, high_ref, low_ref, out_ref):
    columns, _, lat = out_ref.shape
    for x in range(columns):
        cell = first + x * lat + lax.broadcasted_iota(jnp.int32, (code_ref.shape[0], lat), 1)
        hot = jnp.where(code_ref[...] == cell, 1.0, 0.0).astype(jnp.bfloat16)
        total = jnp.dot(high_ref[...], hot, preferred_element_type=jnp.float32)
        out_ref[x] = total + jnp.dot(low_ref[...], hot, preferred_element_type=jnp.float32)


def step_forcing(code, high, low, first, columns, lat):
    payload, slots = high.shape
    vmem = pl.BlockSpec(memory_space=pltpu.VMEM)
    return pl.pallas_call(
        functools.partial(forcing_kernel, first),
        out_shape=jax.ShapeDtypeStruct((columns, payload, lat), jnp.float32),
        in_specs=[vmem] * 3,
        out_specs=vmem,
        compiler_params=pltpu.CompilerParams(vmem_limit_bytes=24 << 20),
        cost_estimate=pl.CostEstimate(
            flops=4 * payload * slots * columns * lat,
            bytes_accessed=4 * payload * (slots + columns * lat),
            transcendentals=0,
        ),
    )(code, high, low)


def split(values):
    high = lax.reduce_precision(values, 8, 7)
    return high.astype(jnp.bfloat16), (values - high).astype(jnp.bfloat16)


def body(
    adjoint_final, winds, diffusivity, observed_values, observed_band, observed_cell, observed_step
):
    tracers, levels, columns, lat = adjoint_final.shape
    steps = winds.shape[0]
    rows, payload = observed_values.shape
    bands = lax.axis_size("lon")
    capacity = max(2, (2 * rows + bands - 1) // bands)
    cells = columns * lat

    target = observed_band[:, 0]
    named = target[:, None] == jnp.arange(bands, dtype=jnp.int32)[None, :]
    counted = named.astype(jnp.float32)
    earlier = (jnp.arange(rows)[:, None] > jnp.arange(rows)[None, :]).astype(jnp.float32)
    before = jnp.dot(earlier, counted, preferred_element_type=jnp.float32)
    slot = jnp.sum(before * counted, axis=1).astype(jnp.int32)
    place = target * capacity + slot
    hot = place[:, None] == jnp.arange(bands * capacity, dtype=jnp.int32)[None, :]
    code = (observed_step * cells + observed_cell).astype(jnp.float32)
    send_code = jnp.sum(jnp.where(hot, code[:, None] + 1.0, 0.0), axis=0) - 1.0
    column = jnp.arange(payload, dtype=jnp.int32)
    source = (column % tracers) * levels + column // tracers
    swap = (column[:, None] == source[None, :]).astype(jnp.bfloat16)
    high, low = split(observed_values)
    dims = (((0,), (0,)), ((), ()))
    send_values = 0.0
    for part in (high, low):
        part = jnp.dot(part, swap, preferred_element_type=jnp.float32).astype(jnp.bfloat16)
        send_values = send_values + lax.dot_general(
            hot.astype(jnp.bfloat16), part, dims, preferred_element_type=jnp.float32
        )

    lat_rows = winds.shape[3]
    parts = winds.reshape(steps * 2 * levels * lat_rows, bands, columns).transpose(1, 0, 2)
    small = jnp.concatenate(
        [parts.reshape(bands, -1), send_code.reshape(bands, capacity)], axis=1
    )
    length = small.shape[1]
    extra = -(-length // payload)
    small = jnp.pad(small, ((0, 0), (0, extra * payload - length)))
    sent = jnp.concatenate(
        [send_values.reshape(bands, capacity, payload), small.reshape(bands, extra, payload)],
        axis=1,
    )
    received = lax.all_to_all(sent, "lon", split_axis=0, concat_axis=0, tiled=True)
    recv_values = received[:, :capacity].reshape(-1, payload)
    small = received[:, capacity:].reshape(bands, extra * payload)[:, :length]
    recv_code = small[:, -capacity:].reshape(-1).astype(jnp.int32)
    own = small[:, :-capacity].reshape(bands, steps, 2, levels, lat_rows, columns)
    own = own.transpose(1, 2, 3, 5, 0, 4).reshape(steps, 2, levels, columns, lat)
    weights = step_weights(own)

    high, low = split(recv_values.T)
    code = recv_code[:, None]

    field = adjoint_final.transpose(1, 2, 0, 3)
    ends = []
    start = 0
    for size in chunk_sizes(tracers):
        ends.append((start, start + size))
        start += size
    states = [(field[:, :, a:b], None, None) for a, b in ends]
    for number, s in enumerate(reversed(range(steps))):
        moved = []
        forcing = step_forcing(code, high, low, s * cells, columns, lat)
        forcing = forcing.reshape(columns, levels, tracers, lat)
        for (a, b), (q, halos, flux) in zip(ends, states):
            if number == 1:
                flux = jnp.zeros((columns, b - a, lat), jnp.float32)
            out = step(q, halos, flux, forcing, weights[s], diffusivity, a)
            halos = (shifted(out[1], "lon", 1), shifted(out[2], "lon", -1))
            moved.append((out[0], halos, out[3] if number else None))
        states = moved
    fields, fluxes = [], []
    for q, halos, flux in states:
        q = q.at[:, 0:2].add(halos[0])
        q = q.at[:, columns - 2 : columns].add(halos[1])
        fields.append(q)
        fluxes.append(flux + q[0])
    field = jnp.concatenate(fields, axis=2).transpose(2, 0, 1, 3)
    return field, jnp.concatenate(fluxes, axis=1).transpose(1, 0, 2)


def solution(mesh):
    return jax.shard_map(
        body,
        mesh=mesh,
        in_specs=(
            P("grp", None, "lon", None),
            P(None, None, None, "lon", None),
            P(None, "lon", None),
            P(("grp", "lon"), None),
            P(("grp", "lon"), None),
            P(("grp", "lon")),
            P(("grp", "lon")),
        ),
        out_specs=(P("grp", None, "lon", None), P("grp", "lon", None)),
        check_vma=False,
    )
```

```python
import functools

import jax
import jax.numpy as jnp
from jax import lax
from jax.experimental import pallas as pl
from jax.experimental.pallas import tpu as pltpu
from jax.sharding import PartitionSpec as P

SUB = 4
ROWS = 8


def chunk_sizes(tracers):
    units = tracers // ROWS
    first = (units + 1) // 2
    return [n * ROWS for n in (first, units - first) if n]


def shifted(block, axis, distance):
    devices = range(lax.axis_size(axis))
    route = [((i - distance) % len(devices), i) for i in devices]
    return lax.ppermute(block, axis, route)


def step_weights(winds):
    u, v = winds[:, 0], winds[:, 1]

    def upwind(c):
        m = jnp.abs(c)
        return [
            -(c + m) / 12.0,
            (8.0 * c + 4.0 * m) / 12.0,
            (4.0 * m - 8.0 * c) / 12.0,
            (c - m) / 12.0,
        ]

    lat = winds.shape[-1]
    place = jnp.arange(lat)
    inside = [
        jnp.where((place + k >= 0) & (place + k < lat), w, 0.0)
        for k, w in zip((-2, -1, 1, 2), upwind(v))
    ]
    centre = 1.0 - 0.5 * jnp.abs(u) - 0.5 * jnp.abs(v)
    return jnp.stack([centre] + inside + upwind(u), axis=1)


def step_kernel(halo, start, *refs):
    if halo:
        q_ref, west_ref, east_ref, flux_ref, f_ref, w_ref, r_ref = refs[:7]
        out_ref, oeast_ref, owest_ref, oflux_ref = refs[7:]
    else:
        q_ref, f_ref, w_ref, r_ref = refs[:4]
        out_ref, oeast_ref, owest_ref = refs[4:]
    levels, columns, tracers, lat = q_ref.shape

    @pl.loop(0, tracers // ROWS)
    def _(i):
        at = pl.ds(pl.multiple_of(i * ROWS, ROWS), ROWS)
        own = pl.ds(pl.multiple_of(start + i * ROWS, ROWS), ROWS)
        for x in range(columns):
            q = [q_ref[l, x, at, :] for l in range(levels)]
            if halo:
                q = [q[l] + (west_ref[l, x, at, :] + east_ref[l, x, at, :]) for l in range(levels)]
                oflux_ref[x, at, :] = flux_ref[x, at, :] + q[0]
            q = [q[l] + f_ref[x, l, own, :] for l in range(levels)]
            for _ in range(SUB):
                flow = [r_ref[l, x : x + 1, :] * (q[l + 1] - q[l]) for l in range(levels - 1)]
                q = (
                    [q[0] + flow[0]]
                    + [q[l] + flow[l] - flow[l - 1] for l in range(1, levels - 1)]
                    + [q[levels - 1] - flow[levels - 2]]
                )
            for l in range(levels):
                out_ref[l, x, at, :] = q[l]
        for l in range(levels):
            q = [out_ref[l, x, at, :] for x in range(columns)]

            def w(k, x):
                return w_ref[k, l, x : x + 1, :]

            total = []
            for x in range(columns):
                t = w(0, x) * q[x]
                for k, offset in ((1, -2), (2, -1), (3, 1), (4, 2)):
                    t = t + pltpu.roll(w(k, x) * q[x], offset % lat, 1)
                total.append(t)
            last = columns - 1
            for k, offset in ((5, -2), (6, -1), (7, 1), (8, 2)):
                for x in range(columns):
                    if 0 <= x + offset < columns:
                        total[x + offset] = total[x + offset] + w(k, x) * q[x]
            for x in range(columns):
                out_ref[l, x, at, :] = total[x]
            oeast_ref[l, 0, at, :] = w(7, last) * q[last] + w(8, last - 1) * q[last - 1]
            oeast_ref[l, 1, at, :] = w(8, last) * q[last]
            owest_ref[l, 0, at, :] = w(5, 0) * q[0]
            owest_ref[l, 1, at, :] = w(6, 0) * q[0] + w(5, 1) * q[1]


def step(q, halos, flux, forcing, weights, rate, start):
    levels, columns, tracers, lat = q.shape
    whole = jax.ShapeDtypeStruct(q.shape, jnp.float32)
    edge = jax.ShapeDtypeStruct((levels, 2, tracers, lat), jnp.float32)
    outs = [whole, edge, edge]
    operands = [q]
    if halos:
        operands += [halos[0], halos[1], flux]
        outs.append(jax.ShapeDtypeStruct(flux.shape, jnp.float32))
    operands += [forcing, weights, rate]
    vmem = pl.BlockSpec(memory_space=pltpu.VMEM)
    size = q.size
    return pl.pallas_call(
        functools.partial(step_kernel, bool(halos), start),
        out_shape=outs,
        in_specs=[vmem] * len(operands),
        out_specs=[vmem] * len(outs),
        compiler_params=pltpu.CompilerParams(vmem_limit_bytes=24 << 20),
        cost_estimate=pl.CostEstimate(flops=60 * size, bytes_accessed=32 * size, transcendentals=0),
    )(*operands)


def forcing_kernel(first, code_ref, high_ref, low_ref, out_ref):
    columns, _, lat = out_ref.shape
    for x in range(columns):
        cell = first + x * lat + lax.broadcasted_iota(jnp.int32, (code_ref.shape[0], lat), 1)
        hot = jnp.where(code_ref[...] == cell, 1.0, 0.0).astype(jnp.bfloat16)
        total = jnp.dot(high_ref[...], hot, preferred_element_type=jnp.float32)
        out_ref[x] = total + jnp.dot(low_ref[...], hot, preferred_element_type=jnp.float32)


def step_forcing(code, high, low, first, columns, lat):
    payload, slots = high.shape
    vmem = pl.BlockSpec(memory_space=pltpu.VMEM)
    return pl.pallas_call(
        functools.partial(forcing_kernel, first),
        out_shape=jax.ShapeDtypeStruct((columns, payload, lat), jnp.float32),
        in_specs=[vmem] * 3,
        out_specs=vmem,
        compiler_params=pltpu.CompilerParams(vmem_limit_bytes=24 << 20),
        cost_estimate=pl.CostEstimate(
            flops=4 * payload * slots * columns * lat,
            bytes_accessed=4 * payload * (slots + columns * lat),
            transcendentals=0,
        ),
    )(code, high, low)


def split(values):
    high = lax.reduce_precision(values, 8, 7)
    return high.astype(jnp.bfloat16), (values - high).astype(jnp.bfloat16)


def body(
    adjoint_final, winds, diffusivity, observed_values, observed_band, observed_cell, observed_step
):
    tracers, levels, columns, lat = adjoint_final.shape
    steps = winds.shape[0]
    rows, payload = observed_values.shape
    bands = lax.axis_size("lon")
    capacity = max(2, (2 * rows + bands - 1) // bands)
    cells = columns * lat

    target = observed_band[:, 0]
    named = target[:, None] == jnp.arange(bands, dtype=jnp.int32)[None, :]
    counted = named.astype(jnp.float32)
    earlier = (jnp.arange(rows)[:, None] > jnp.arange(rows)[None, :]).astype(jnp.float32)
    before = jnp.dot(earlier, counted, preferred_element_type=jnp.float32)
    slot = jnp.sum(before * counted, axis=1).astype(jnp.int32)
    place = target * capacity + slot
    hot = place[:, None] == jnp.arange(bands * capacity, dtype=jnp.int32)[None, :]
    code = (observed_step * cells + observed_cell).astype(jnp.float32)
    send_code = jnp.sum(jnp.where(hot, code[:, None] + 1.0, 0.0), axis=0) - 1.0
    column = jnp.arange(payload, dtype=jnp.int32)
    source = (column % tracers) * levels + column // tracers
    swap = (column[:, None] == source[None, :]).astype(jnp.bfloat16)
    high, low = split(observed_values)
    dims = (((0,), (0,)), ((), ()))
    send_values = 0.0
    for part in (high, low):
        part = jnp.dot(part, swap, preferred_element_type=jnp.float32).astype(jnp.bfloat16)
        send_values = send_values + lax.dot_general(
            hot.astype(jnp.bfloat16), part, dims, preferred_element_type=jnp.float32
        )

    lat_rows = winds.shape[3]
    parts = winds.reshape(steps * 2 * levels * lat_rows, bands, columns).transpose(1, 0, 2)
    small = jnp.concatenate(
        [parts.reshape(bands, -1), send_code.reshape(bands, capacity)], axis=1
    )
    recv_values = lax.all_to_all(send_values, "lon", split_axis=0, concat_axis=0, tiled=True)
    recv_values, small = lax.optimization_barrier((recv_values, small))
    small = lax.all_to_all(small, "lon", split_axis=0, concat_axis=0, tiled=True)
    recv_code = small[:, -capacity:].reshape(-1).astype(jnp.int32)
    own = small[:, :-capacity].reshape(bands, steps, 2, levels, lat_rows, columns)
    own = own.transpose(1, 2, 3, 5, 0, 4).reshape(steps, 2, levels, columns, lat)
    weights = step_weights(own)

    high, low = split(recv_values.T)
    code = recv_code[:, None]

    field = adjoint_final.transpose(1, 2, 0, 3)
    ends = []
    start = 0
    for size in chunk_sizes(tracers):
        ends.append((start, start + size))
        start += size
    states = [(field[:, :, a:b], None, None) for a, b in ends]
    for number, s in enumerate(reversed(range(steps))):
        moved = []
        forcing = step_forcing(code, high, low, s * cells, columns, lat)
        forcing = forcing.reshape(columns, levels, tracers, lat)
        for (a, b), (q, halos, flux) in zip(ends, states):
            if number == 1:
                flux = jnp.zeros((columns, b - a, lat), jnp.float32)
            out = step(q, halos, flux, forcing, weights[s], diffusivity, a)
            halos = (shifted(out[1], "lon", 1), shifted(out[2], "lon", -1))
            moved.append((out[0], halos, out[3] if number else None))
        states = moved
    fields, fluxes = [], []
    for q, halos, flux in states:
        q = q.at[:, 0:2].add(halos[0])
        q = q.at[:, columns - 2 : columns].add(halos[1])
        fields.append(q)
        fluxes.append(flux + q[0])
    field = jnp.concatenate(fields, axis=2).transpose(2, 0, 1, 3)
    return field, jnp.concatenate(fluxes, axis=1).transpose(1, 0, 2)


def solution(mesh):
    return jax.shard_map(
        body,
        mesh=mesh,
        in_specs=(
            P("grp", None, "lon", None),
            P(None, None, None, "lon", None),
            P(None, "lon", None),
            P(("grp", "lon"), None),
            P(("grp", "lon"), None),
            P(("grp", "lon")),
            P(("grp", "lon")),
        ),
        out_specs=(P("grp", None, "lon", None), P("grp", "lon", None)),
        check_vma=False,
    )
```

```python
import functools

import jax
import jax.numpy as jnp
from jax import lax
from jax.experimental import pallas as pl
from jax.experimental.pallas import tpu as pltpu
from jax.sharding import PartitionSpec as P

SUB = 4
ROWS = 8


def chunk_sizes(tracers):
    units = tracers // ROWS
    return [units * ROWS * (i + 1) // 3 // ROWS * ROWS - units * ROWS * i // 3 // ROWS * ROWS
            for i in range(3)]


def shifted(block, axis, distance):
    devices = range(lax.axis_size(axis))
    route = [((i - distance) % len(devices), i) for i in devices]
    return lax.ppermute(block, axis, route)


def step_weights(winds):
    u, v = winds[:, 0], winds[:, 1]

    def upwind(c):
        m = jnp.abs(c)
        return [
            -(c + m) / 12.0,
            (8.0 * c + 4.0 * m) / 12.0,
            (4.0 * m - 8.0 * c) / 12.0,
            (c - m) / 12.0,
        ]

    lat = winds.shape[-1]
    place = jnp.arange(lat)
    inside = [
        jnp.where((place + k >= 0) & (place + k < lat), w, 0.0)
        for k, w in zip((-2, -1, 1, 2), upwind(v))
    ]
    centre = 1.0 - 0.5 * jnp.abs(u) - 0.5 * jnp.abs(v)
    return jnp.stack([centre] + inside + upwind(u), axis=1)


def step_kernel(halo, start, *refs):
    if halo:
        q_ref, west_ref, east_ref, flux_ref, f_ref, w_ref, r_ref = refs[:7]
        out_ref, oeast_ref, owest_ref, oflux_ref = refs[7:]
    else:
        q_ref, f_ref, w_ref, r_ref = refs[:4]
        out_ref, oeast_ref, owest_ref = refs[4:]
    levels, columns, tracers, lat = q_ref.shape

    @pl.loop(0, tracers // ROWS)
    def _(i):
        at = pl.ds(pl.multiple_of(i * ROWS, ROWS), ROWS)
        own = pl.ds(pl.multiple_of(start + i * ROWS, ROWS), ROWS)
        for x in range(columns):
            q = [q_ref[l, x, at, :] for l in range(levels)]
            if halo:
                q = [q[l] + (west_ref[l, x, at, :] + east_ref[l, x, at, :]) for l in range(levels)]
                oflux_ref[x, at, :] = flux_ref[x, at, :] + q[0]
            q = [q[l] + f_ref[x, l, own, :] for l in range(levels)]
            for _ in range(SUB):
                flow = [r_ref[l, x : x + 1, :] * (q[l + 1] - q[l]) for l in range(levels - 1)]
                q = (
                    [q[0] + flow[0]]
                    + [q[l] + flow[l] - flow[l - 1] for l in range(1, levels - 1)]
                    + [q[levels - 1] - flow[levels - 2]]
                )
            for l in range(levels):
                out_ref[l, x, at, :] = q[l]
        for l in range(levels):
            q = [out_ref[l, x, at, :] for x in range(columns)]

            def w(k, x):
                return w_ref[k, l, x : x + 1, :]

            total = []
            for x in range(columns):
                t = w(0, x) * q[x]
                for k, offset in ((1, -2), (2, -1), (3, 1), (4, 2)):
                    t = t + pltpu.roll(w(k, x) * q[x], offset % lat, 1)
                total.append(t)
            last = columns - 1
            for k, offset in ((5, -2), (6, -1), (7, 1), (8, 2)):
                for x in range(columns):
                    if 0 <= x + offset < columns:
                        total[x + offset] = total[x + offset] + w(k, x) * q[x]
            for x in range(columns):
                out_ref[l, x, at, :] = total[x]
            oeast_ref[l, 0, at, :] = w(7, last) * q[last] + w(8, last - 1) * q[last - 1]
            oeast_ref[l, 1, at, :] = w(8, last) * q[last]
            owest_ref[l, 0, at, :] = w(5, 0) * q[0]
            owest_ref[l, 1, at, :] = w(6, 0) * q[0] + w(5, 1) * q[1]


def step(q, halos, flux, forcing, weights, rate, start):
    levels, columns, tracers, lat = q.shape
    whole = jax.ShapeDtypeStruct(q.shape, jnp.float32)
    edge = jax.ShapeDtypeStruct((levels, 2, tracers, lat), jnp.float32)
    outs = [whole, edge, edge]
    operands = [q]
    if halos:
        operands += [halos[0], halos[1], flux]
        outs.append(jax.ShapeDtypeStruct(flux.shape, jnp.float32))
    operands += [forcing, weights, rate]
    vmem = pl.BlockSpec(memory_space=pltpu.VMEM)
    size = q.size
    return pl.pallas_call(
        functools.partial(step_kernel, bool(halos), start),
        out_shape=outs,
        in_specs=[vmem] * len(operands),
        out_specs=[vmem] * len(outs),
        compiler_params=pltpu.CompilerParams(vmem_limit_bytes=24 << 20),
        cost_estimate=pl.CostEstimate(flops=60 * size, bytes_accessed=32 * size, transcendentals=0),
    )(*operands)


def forcing_kernel(first, code_ref, high_ref, low_ref, out_ref):
    columns, _, lat = out_ref.shape
    for x in range(columns):
        cell = first + x * lat + lax.broadcasted_iota(jnp.int32, (code_ref.shape[0], lat), 1)
        hot = jnp.where(code_ref[...] == cell, 1.0, 0.0).astype(jnp.bfloat16)
        total = jnp.dot(high_ref[...], hot, preferred_element_type=jnp.float32)
        out_ref[x] = total + jnp.dot(low_ref[...], hot, preferred_element_type=jnp.float32)


def step_forcing(code, high, low, first, columns, lat):
    payload, slots = high.shape
    vmem = pl.BlockSpec(memory_space=pltpu.VMEM)
    return pl.pallas_call(
        functools.partial(forcing_kernel, first),
        out_shape=jax.ShapeDtypeStruct((columns, payload, lat), jnp.float32),
        in_specs=[vmem] * 3,
        out_specs=vmem,
        compiler_params=pltpu.CompilerParams(vmem_limit_bytes=24 << 20),
        cost_estimate=pl.CostEstimate(
            flops=4 * payload * slots * columns * lat,
            bytes_accessed=4 * payload * (slots + columns * lat),
            transcendentals=0,
        ),
    )(code, high, low)


def split(values):
    high = lax.reduce_precision(values, 8, 7)
    return high.astype(jnp.bfloat16), (values - high).astype(jnp.bfloat16)


def body(
    adjoint_final, winds, diffusivity, observed_values, observed_band, observed_cell, observed_step
):
    tracers, levels, columns, lat = adjoint_final.shape
    steps = winds.shape[0]
    rows, payload = observed_values.shape
    bands = lax.axis_size("lon")
    capacity = max(2, (2 * rows + bands - 1) // bands)
    cells = columns * lat

    target = observed_band[:, 0]
    named = target[:, None] == jnp.arange(bands, dtype=jnp.int32)[None, :]
    counted = named.astype(jnp.float32)
    earlier = (jnp.arange(rows)[:, None] > jnp.arange(rows)[None, :]).astype(jnp.float32)
    before = jnp.dot(earlier, counted, preferred_element_type=jnp.float32)
    slot = jnp.sum(before * counted, axis=1).astype(jnp.int32)
    place = target * capacity + slot
    hot = place[:, None] == jnp.arange(bands * capacity, dtype=jnp.int32)[None, :]
    code = (observed_step * cells + observed_cell).astype(jnp.float32)
    send_code = jnp.sum(jnp.where(hot, code[:, None] + 1.0, 0.0), axis=0) - 1.0
    column = jnp.arange(payload, dtype=jnp.int32)
    source = (column % tracers) * levels + column // tracers
    swap = (column[:, None] == source[None, :]).astype(jnp.bfloat16)
    high, low = split(observed_values)
    dims = (((0,), (0,)), ((), ()))
    send_values = 0.0
    for part in (high, low):
        part = jnp.dot(part, swap, preferred_element_type=jnp.float32).astype(jnp.bfloat16)
        send_values = send_values + lax.dot_general(
            hot.astype(jnp.bfloat16), part, dims, preferred_element_type=jnp.float32
        )

    lat_rows = winds.shape[3]
    parts = winds.reshape(steps * 2 * levels * lat_rows, bands, columns).transpose(1, 0, 2)
    small = jnp.concatenate(
        [parts.reshape(bands, -1), send_code.reshape(bands, capacity)], axis=1
    )
    small = lax.all_to_all(small, "lon", split_axis=0, concat_axis=0, tiled=True)
    recv_values = lax.all_to_all(send_values, "lon", split_axis=0, concat_axis=0, tiled=True)
    recv_code = small[:, -capacity:].reshape(-1).astype(jnp.int32)
    own = small[:, :-capacity].reshape(bands, steps, 2, levels, lat_rows, columns)
    own = own.transpose(1, 2, 3, 5, 0, 4).reshape(steps, 2, levels, columns, lat)
    weights = step_weights(own)

    high, low = split(recv_values.T)
    code = recv_code[:, None]

    field = adjoint_final.transpose(1, 2, 0, 3)
    ends = []
    start = 0
    for size in chunk_sizes(tracers):
        ends.append((start, start + size))
        start += size
    states = [(field[:, :, a:b], None, None) for a, b in ends]
    for number, s in enumerate(reversed(range(steps))):
        moved = []
        forcing = step_forcing(code, high, low, s * cells, columns, lat)
        forcing = forcing.reshape(columns, levels, tracers, lat)
        for (a, b), (q, halos, flux) in zip(ends, states):
            if number == 1:
                flux = jnp.zeros((columns, b - a, lat), jnp.float32)
            out = step(q, halos, flux, forcing, weights[s], diffusivity, a)
            halos = (shifted(out[1], "lon", 1), shifted(out[2], "lon", -1))
            moved.append((out[0], halos, out[3] if number else None))
        states = moved
    fields, fluxes = [], []
    for q, halos, flux in states:
        q = q.at[:, 0:2].add(halos[0])
        q = q.at[:, columns - 2 : columns].add(halos[1])
        fields.append(q)
        fluxes.append(flux + q[0])
    field = jnp.concatenate(fields, axis=2).transpose(2, 0, 1, 3)
    return field, jnp.concatenate(fluxes, axis=1).transpose(1, 0, 2)


def solution(mesh):
    return jax.shard_map(
        body,
        mesh=mesh,
        in_specs=(
            P("grp", None, "lon", None),
            P(None, None, None, "lon", None),
            P(None, "lon", None),
            P(("grp", "lon"), None),
            P(("grp", "lon"), None),
            P(("grp", "lon")),
            P(("grp", "lon")),
        ),
        out_specs=(P("grp", None, "lon", None), P("grp", "lon", None)),
        check_vma=False,
    )
```
